256 devices in a mesh: clus: 128 (over x, z, y), rhs: 2 (over core).
Axes of the slice: x: 4, y: 4, z: 8, core: 2. Of those that a mesh axis runs over, the one named last changes fastest.
Arguments:
- centers: bfloat16 [3, 1048576], P(None, 'clus'), may hold values from -5 to 5
- normals: bfloat16 [3, 1048576], P(None, 'clus'), may hold values from -1 to 1
- weights: bfloat16 [1048576], P('clus'), may hold values from 0.5 to 2
- density: bfloat16 [32, 1048576], P('rhs', 'clus'), may hold values from -6 to 6
- near_pairs: int32 [2, 2, 2048], P(None, None, 'clus'), may hold values from 0 to 15, as said below
- parent: int32 [2048], P('clus'), may hold values from 0 to 7
- far_src: int32 [1024, 32], P('clus'), may hold values from 0 to 1023
- src_basis: bfloat16 [2048, 32, 512], P('clus'), may hold values from -0.25 to 0.25
- upward_transfer: float32 [2048, 32, 32], P('clus'), may hold values from -1 to 1
- far_mat: bfloat16 [1024, 32, 1024], P('clus'), may hold values from -0.1875 to 0.1875
- downward_transfer: float32 [2048, 32, 32], P('clus'), may hold values from -1 to 1
- tgt_basis: bfloat16 [2048, 32, 512], P('clus'), may hold values from -1 to 1
Outputs:
- potential: float32 [32, 1048576], P('rhs', 'clus')
The draws below stay inside these ranges and needn't reach their ends.
Inputs may be any that keep to these rules, and one draw needn't show every extreme that they name: `near_pairs`: for each device and offset the targets name each of the device's 16 clusters once, and the sources name exactly 8 distinct clusters.
All inputs are finite; a program needn't handle non-finite values.
Results may differ from the reference program's by a relative error of at most 0.0029.
Values may be sent and summed in bfloat16 or wider, within the bound.
A program may use at most 64 MiB of HBM per device.

```python
import math
import jax
import jax.numpy as jnp
from jax import lax

CL_DEV = 16
P_SIZE = 512
RANK = 32
RHS = 32
W = 2
FAR = 32
TOP_DEV = 8
CAP = 8
NCL = 2048
NTOP = 1024
PANELS = 1048576


def draw_near_pairs(key, part):
    key = jax.random.fold_in(key, 11)
    key_one, key_two = jax.random.split(key)
    devices = NCL // CL_DEV
    slot_ids = jnp.arange(CL_DEV, dtype=jnp.int32)
    scores_one = jax.random.randint(key_one, (W, devices, CL_DEV), 0, 1 << 20) * CL_DEV + slot_ids
    targets = jnp.argsort(scores_one, axis=-1).astype(jnp.int32)
    scores_two = jax.random.randint(key_two, (W, devices, CL_DEV), 0, 1 << 20) * CL_DEV + slot_ids
    chosen = jnp.argsort(scores_two, axis=-1).astype(jnp.int32)[..., :CAP]
    picks = jnp.broadcast_to(slot_ids % CAP, (W, devices, CL_DEV))
    sources = jnp.take_along_axis(chosen, picks, axis=-1).astype(jnp.int32)
    return jnp.stack([targets, sources]).reshape(2, W, NCL)


def touch_ends(values, stream_key, least, top_value):
    longest = values.shape.index(max(values.shape))
    spots = []
    for shift in (0, 1):
        where = [jax.random.randint(jax.random.fold_in(stream_key, axis), (), 0, length) for axis, length in enumerate(values.shape)]
        where[longest] = (where[longest] + shift) % values.shape[longest]
        spots.append(tuple(where))
    return values.at[spots[0]].set(least).at[spots[1]].set(top_value)


def steps_of(own_key, shape, cuts, low, high):
    loudness, own = 1.0, jax.random.fold_in(own_key, 6)
    for axis_at, blocks in cuts:
        draws = jnp.exp(jax.random.uniform(jax.random.fold_in(own, axis_at), (blocks,), jnp.float32, low / len(cuts), high / len(cuts)))
        loudness = loudness * jnp.repeat(draws, shape[axis_at] // blocks).reshape([-1 if axis == axis_at else 1 for axis in range(len(shape))])
    return loudness


def normal_values(own_key, dims, deviation, reach, pieces=(), kind=jnp.bfloat16):
    factor_of = steps_of(own_key, dims, pieces, -0.22, 0.18) if pieces else 1.0
    drawn = jax.random.normal(own_key, dims, jnp.float32) * deviation * factor_of
    return jnp.minimum(jnp.maximum(drawn, -reach), reach).astype(kind)


def setup_inputs(seed: int = 0) -> dict:
    arg_keys = jax.random.split(jax.random.key(seed), 13)
    return {
        "centers": normal_values(arg_keys[0], (3, PANELS), 1.0, 5.0, ((1, 128),)),
        "normals": jnp.clip(jax.random.uniform(arg_keys[1], (3, PANELS), jnp.float32, -1.0, 1.0) * steps_of(arg_keys[1], (3, PANELS), ((1, 128),), -0.4, 0.0), -1.0, 1.0).astype(jnp.bfloat16),
        "weights": jnp.clip(jnp.exp(math.log(2.0) - 1.3862944 * jax.random.uniform(arg_keys[2], (PANELS,), jnp.float32) ** steps_of(arg_keys[2], (PANELS,), ((0, 128),), -0.2, 0.2)), 0.5, 2.0).astype(jnp.bfloat16),
        "density": normal_values(arg_keys[3], (RHS, PANELS), 1.0, 6.0, ((0, 2), (1, 128))),
        "near_pairs": draw_near_pairs(jax.random.fold_in(arg_keys[12], 71), 0),
        "parent": touch_ends(jax.random.randint(arg_keys[5], (NCL,), 0, TOP_DEV), jax.random.fold_in(arg_keys[5], 1), 0, TOP_DEV - 1).astype(jnp.int32),
        "far_src": touch_ends(jax.random.randint(arg_keys[6], (NTOP, FAR), 0, NTOP), jax.random.fold_in(arg_keys[6], 1), 0, NTOP - 1).astype(jnp.int32),
        "src_basis": normal_values(arg_keys[7], (NCL, RANK, P_SIZE), P_SIZE ** -0.5, 0.25, ((0, 128),)),
        "upward_transfer": normal_values(arg_keys[8], (NCL, RANK, RANK), RANK ** -0.5, 1.0, ((0, 128),), jnp.float32),
        "far_mat": normal_values(arg_keys[9], (NTOP, RANK, FAR * RANK), (FAR * RANK) ** -0.5, 0.1875, ((0, 128),)),
        "downward_transfer": normal_values(arg_keys[10], (NCL, RANK, RANK), RANK ** -0.5, 1.0, ((0, 128),), jnp.float32),
        "tgt_basis": normal_values(arg_keys[11], (NCL, RANK, P_SIZE), RANK ** -0.5, 1.0, ((0, 128),)),
    }


DELTA2 = 0.25
MAX_PRECISION = lax.Precision.HIGHEST

def panel_tiles(tgt_geo, src_geo):
    tgt_geo = tgt_geo.astype(jnp.float32)
    src_geo = src_geo.astype(jnp.float32)
    delta_xyz = tgt_geo[0:3, :, None] - src_geo[0:3, None, :]
    dist_sq = lax.optimization_barrier(jnp.sum(delta_xyz * delta_xyz, axis=0)) + DELTA2
    kernel_scale = tgt_geo[6][:, None] * src_geo[6][None, :] / (dist_sq * jnp.sqrt(dist_sq))
    forward = (lax.optimization_barrier(jnp.sum(src_geo[3:6][:, None, :] * delta_xyz, axis=0)) * kernel_scale).astype(jnp.bfloat16)
    backward = (-lax.optimization_barrier(jnp.sum(tgt_geo[3:6][:, :, None] * delta_xyz, axis=0)) * kernel_scale).astype(jnp.bfloat16)
    return (forward, backward)

def index_cluster(array, cluster):
    return lax.dynamic_index_in_dim(array, cluster, 1, keepdims=False)

def add_cluster(running, addend, cluster):
    return lax.dynamic_update_index_in_dim(running, index_cluster(running, cluster) + addend, cluster, 1)

def reference(centers, normals, weights, density, near_pairs, parent, far_src, src_basis, upward_transfer, far_mat, downward_transfer, tgt_basis):
    devices = NCL // CL_DEV
    geometry = jnp.concatenate([centers, normals, weights[None, :]], axis=0).reshape(7, NCL, P_SIZE)
    columns = density.reshape(RHS, NCL, P_SIZE)
    running = jnp.zeros((RHS, NCL, P_SIZE), jnp.float32)

    def self_block(running, cluster):
        tgt_geo = index_cluster(geometry, cluster)
        forward, unused = panel_tiles(tgt_geo, tgt_geo)
        src_cols = index_cluster(columns, cluster)
        return (add_cluster(running, jnp.dot(src_cols, forward.T, preferred_element_type=jnp.float32), cluster), None)
    running, unused = lax.scan(self_block, running, jnp.arange(NCL, dtype=jnp.int32))
    owner_dev = jnp.arange(NCL, dtype=jnp.int32) // CL_DEV
    firsts, seconds, valids = ([], [], [])
    for offset in range(1, W + 1):
        inside = owner_dev + offset < devices
        firsts.append((owner_dev * CL_DEV + near_pairs[0, offset - 1]).astype(jnp.int32))
        seconds.append(jnp.where(inside, (owner_dev + offset) * CL_DEV + near_pairs[1, offset - 1], 0).astype(jnp.int32))
        valids.append(inside.astype(jnp.float32))

    def cross(running, pair_item):
        target, source, is_live = pair_item
        forward, backward = panel_tiles(index_cluster(geometry, target), index_cluster(geometry, source))
        to_target = jnp.dot(index_cluster(columns, source), forward.T, preferred_element_type=jnp.float32)
        running = add_cluster(running, is_live * to_target, target)
        to_source = jnp.dot(index_cluster(columns, target), backward, preferred_element_type=jnp.float32)
        running = add_cluster(running, is_live * to_source, source)
        return (running, None)
    running, unused = lax.scan(cross, running, (jnp.concatenate(firsts), jnp.concatenate(seconds), jnp.concatenate(valids)))
    leaf_coefficient = jnp.einsum('crp,ncp->crn', src_basis.astype(jnp.float32), columns.astype(jnp.float32), precision=MAX_PRECISION)
    child_coefficient = jnp.einsum('ypk,ykg->ypg', upward_transfer, leaf_coefficient, precision=MAX_PRECISION)
    top_cluster_index = (owner_dev * TOP_DEV + parent).astype(jnp.int32)
    top_coef = jax.ops.segment_sum(child_coefficient, top_cluster_index, num_segments=NTOP)
    picked = top_coef[far_src.reshape(-1)].reshape(NTOP, FAR * RANK, RHS)
    distant_coefficient = jnp.einsum('tak,tkn->tan', far_mat.astype(jnp.float32), picked, precision=MAX_PRECISION)
    downward_coefficient = jnp.einsum('ypk,ykg->ypg', downward_transfer, distant_coefficient[top_cluster_index], precision=MAX_PRECISION).astype(jnp.bfloat16)
    far_part = jnp.einsum('cap,can->ncp', tgt_basis.astype(jnp.float32), downward_coefficient.astype(jnp.float32), precision=MAX_PRECISION)
    return (running + far_part).reshape(RHS, PANELS)
```

```python
import functools

import jax
import jax.numpy as jnp
from jax import lax
from jax.experimental import pallas as pl
from jax.experimental.pallas import tpu as pltpu
from jax.sharding import PartitionSpec as P

F32 = jnp.float32
BF16 = jnp.bfloat16
MESH = pl.DeviceIdType.MESH
HIGHEST = lax.Precision.HIGHEST

DELTA2 = 0.25
W = 2
X, Z, Y = 4, 8, 4
N = X * Z * Y
CL = 16
HALF = 8
CAP = 8
PS = 512
COLS = 16
RANK = 32
TOPS = 8
FAR = 32

LIST, SLOT, RANKED, PRESENT = 0, 8, 24, 40


def mm(a, b, precision=None):
    return jnp.dot(a, b, preferred_element_type=F32, precision=precision)


def mm_nt(a, b, precision=None):
    return lax.dot_general(
        a, b, (((1,), (1,)), ((), ())), preferred_element_type=F32, precision=precision
    )


def split3(v):
    high = v.astype(BF16).astype(F32)
    rest = v - high
    mid = rest.astype(BF16).astype(F32)
    return high, mid, rest - mid


def features(geo):
    row = lax.broadcasted_iota(jnp.int32, geo.shape, 0)
    low = row < 3
    mid = (row >= 3) & (row < 6)
    w = geo[6:7]
    weighted = geo * w
    xh = weighted.astype(BF16).astype(F32)
    xl = weighted - xh
    yh = jnp.where(low, jnp.roll(xh, -3, axis=0), 0.0)
    yl = jnp.where(low, jnp.roll(xl, -3, axis=0), 0.0)
    c0, c1, c2 = geo[0:1], geo[1:2], geo[2:3]
    square = c0 * c0 + c1 * c1 + c2 * c2 + 0.5 * DELTA2
    offset = -(weighted[3:4] * c0 + weighted[4:5] * c1 + weighted[5:6] * c2)

    def rows_3_to_5(parts, base):
        h, m, l = parts
        return jnp.where(row == 3, h, jnp.where(row == 4, m, jnp.where(row == 5, l, base)))

    sh, sm, sl = split3(square)
    q1 = [
        rows_3_to_5((sh, sm, sl), jnp.where(low, -2.0 * geo, 0.0)),
        jnp.where(low, 1.0, 0.0),
    ]
    q2 = [
        jnp.where(low, geo, jnp.where(mid, 1.0, 0.0)),
        jnp.where(row == 0, sh, jnp.where(row == 1, sm, jnp.where(row == 2, sl, 0.0))),
    ]
    u = [jnp.where(low, xh, jnp.where(mid, w, 0.0)), xl, xh, xl]
    v = [rows_3_to_5(split3(offset), yh), yh, yl, yl]
    return q1, q2, u, v


def target_features(geo):
    q1, q2, u, v = features(geo)
    pad = jnp.zeros((48, PS), F32)
    left = jnp.concatenate(q1 + u + v + [pad], axis=0).T.astype(BF16)
    return left, jnp.concatenate(q2 + v + u, axis=0).astype(BF16)


def source_features(geo):
    q1, q2, u, v = features(geo)
    return jnp.concatenate(q2 + v + u, axis=0).astype(BF16)


def cube(q):
    t = lax.rsqrt(q)
    return t * t * t


def kernel(
    cen, nor, wts, den, idx1, idx2, parent, far_idx, src_basis, up, far_mat, down, tgt_basis,
    out,
    geo, dens, left, right, dsib, sendd, sendg, bown1, bown2, bsib1, bsib2, bgeo1, bgeo2, bright, near, ybuf,
    part_own, part_sib, part_recv, ret_send, ret_recv1, ret_recv2, near_sib, near_recv, table, folded, far_top, ridx1, ridx2,
    s_idx, r_idx, s_sib, r_sib, s_bd, r_bd, s_bg, r_bg, s_fd, r_fd, s_fg, r_fg, s_ps, r_ps,
    s_rt, r_rt, s_nr, r_nr, s_z, r_z, s_y, r_y, s_x, r_x,
):
    me = lax.axis_index("clus")
    core = lax.axis_index("rhs")
    y = lax.rem(me, Y)
    z = lax.rem(me // Y, Z)
    x = me // (Y * Z)
    idx = (idx1, idx2)
    ridx = (ridx1, ridx2)
    bown, bsib, bgeo = (bown1, bown2), (bsib1, bsib2), (bgeo1, bgeo2)
    ret_recv = (ret_recv1, ret_recv2)
    mine = core * HALF
    other = (1 - core) * HALF

    def along(step):
        return {"clus": lax.rem(me + step + N, N)}

    sibling = {"rhs": 1 - core}
    z_peers = [{"clus": (x * Z + lax.rem(z + k, Z)) * Y + y} for k in range(1, Z)]
    y_peers = [{"clus": (x * Z + z) * Y + lax.rem(y + k, Y)} for k in range(1, Y)]
    x_peers = [{"clus": (lax.rem(x + k, X) * Z + z) * Y + y} for k in range(1, X)]

    def remote(src, dst, send, recv, to):
        return pltpu.make_async_remote_copy(
            src_ref=src, dst_ref=dst, send_sem=send, recv_sem=recv, device_id=to, device_id_type=MESH
        )

    barrier = pltpu.get_barrier_semaphore()
    partners = [sibling] + [along(s) for s in (1, 2, -1, -2)] + z_peers + y_peers + x_peers
    for partner in partners:
        pl.semaphore_signal(barrier, inc=1, device_id=partner, device_id_type=MESH)
    pl.semaphore_wait(barrier, len(partners))

    idx_copies = [
        remote(idx[o], ridx[o], s_idx.at[o], r_idx.at[o], along(o + 1)) for o in range(W)
    ]
    for copy in idx_copies:
        copy.start()
    sib_copy = remote(
        den.at[:, pl.ds(pl.multiple_of(other * PS, PS), HALF * PS)], dsib, s_sib, r_sib, sibling
    )
    sib_copy.start()

    for c in range(CL):
        at = pl.ds(c * PS, PS)
        rows = [cen[:, at].astype(F32), nor[:, at].astype(F32), wts[:, at].astype(F32)]
        dens[c] = den[:, at]
        geo[c] = jnp.concatenate(rows + [jnp.zeros((1, PS), F32)], axis=0)

    b_copies = []
    for o in range(W):
        idx_copies[o].wait()
        for m in range(CAP):
            c = ridx[o][LIST + m]
            sendd[o, m] = dens[c]
        for m in range(2):
            c0 = ridx[o][LIST + core * 4 + 2 * m]
            c1 = ridx[o][LIST + core * 4 + 2 * m + 1]
            sendg[o, m] = jnp.concatenate([geo[c0], geo[c1]], axis=0).astype(BF16)
        copies = (
            remote(sendg.at[o], bgeo[o].at[pl.ds(core * 2, 2)], s_bg.at[o], r_bg.at[o], along(-o - 1)),
            remote(sendd.at[o], bown[o], s_bd.at[o], r_bd.at[o], along(-o - 1)),
        )
        for copy in copies:
            copy.start()
        b_copies.append(copies)

    tops = [jnp.zeros((COLS, RANK), F32) for _ in range(TOPS)]
    for c in range(CL):
        leaf = mm_nt(den[:, c * PS : (c + 1) * PS], src_basis[c])
        child = mm_nt(leaf, up[c], HIGHEST)
        for t in range(TOPS):
            tops[t] = tops[t] + jnp.where(parent[c] == t, child, 0.0)
    flat = (x * Y + y) * Z + z
    for h in range(2):
        table[2 * flat + h] = jnp.concatenate(tops[4 * h : 4 * h + 4], axis=1).astype(BF16)

    def gather_step(start, size, peers, send, recv):
        block = table.at[pl.ds(start, size)]
        copies = [
            remote(block, block, send.at[k], recv.at[k], to) for k, to in enumerate(peers)
        ]
        for copy in copies:
            copy.start()
        return copies

    z_copies = gather_step(2 * flat, 2, z_peers, s_z, r_z)

    for t in range(HALF):
        left[t], right[t] = target_features(geo[mine + t])
    sib_copy.wait()
    for copy in z_copies:
        copy.wait()
    y_copies = gather_step((x * Y + y) * Z * 2, Z * 2, y_peers, s_y, r_y)

    def densities(t):
        own = den[:, pl.ds(pl.multiple_of((mine + t) * PS, PS), PS)]
        return jnp.concatenate([own, dsib[:, pl.ds(pl.multiple_of(t * PS, PS), PS)]], axis=0)

    def self_pair(u, carry):
        for k in range(2):
            t = 2 * u + k
            q = mm(left[t, :, 0:16], right[t, 0:16])
            nb = mm(left[t, :, 48:80], right[t, 48:80])
            near[t] = mm(densities(t), (nb * cube(q)).astype(BF16))
        return carry

    lax.fori_loop(0, HALF // 2, self_pair, 0)

    for copy in y_copies:
        copy.wait()
    x_copies = gather_step(x * Y * Z * 2, Y * Z * 2, x_peers, s_x, r_x)

    def arrived(o):
        for copy in b_copies[o]:
            copy.wait()
        half = pl.ds(core * 2, 2)
        forwards = (
            remote(bgeo[o].at[half], bgeo[o].at[half], s_fg.at[o], r_fg.at[o], sibling),
            remote(bown[o], bsib[o], s_fd.at[o], r_fd.at[o], sibling),
        )
        for copy in forwards:
            copy.start()
        return forwards

    def cross(o, forwards):
        for copy in forwards:
            copy.wait()
        for m in range(CAP):
            pair = bgeo[o][m // 2].astype(F32)
            bright[m] = source_features(pair[8 * (m % 2) : 8 * (m % 2) + 8])
        live = jnp.where(me + o + 1 < N, 1.0, 0.0).astype(F32)

        def cross_pair(u, carry):
            for k in range(2):
                t = 2 * u + k
                m = idx[o][SLOT + mine + t]
                q = mm(left[t, :, 0:16], bright[m, 0:16])
                nf = mm(left[t, :, 16:48], bright[m, 16:48])
                nb = mm(left[t, :, 48:80], bright[m, 48:80])
                scale = cube(q)
                there = jnp.concatenate([bown[o][m], bsib[o][m]], axis=0)
                near[t] += live * mm_nt(there, (nf * scale).astype(BF16))
                ybuf[t] = mm(densities(t), (nb * scale).astype(BF16))
            return carry

        lax.fori_loop(0, HALF // 2, cross_pair, 0)
        for rows, dst in ((0, part_own), (COLS, part_sib)):
            for r in range(0, COLS, 8):
                tiles = [ybuf[t, rows + r : rows + r + 8, :] for t in range(HALF)]
                for m in range(CAP):
                    total = None
                    for t in range(HALF):
                        hit = jnp.where(idx[o][SLOT + mine + t] == m, 1.0, 0.0).astype(F32)
                        term = hit * tiles[t]
                        total = term if total is None else total + term
                    dst[o, m, r : r + 8, :] = total
        copy = remote(part_sib.at[o], part_recv.at[o], s_ps.at[o], r_ps.at[o], sibling)
        copy.start()
        return copy

    def send_back(o, copy):
        copy.wait()
        for m in range(CAP):
            ret_send[o, m] = (part_own[o, m] + part_recv[o, m]).astype(BF16)
        back = remote(ret_send.at[o], ret_recv[o], s_rt.at[o], r_rt.at[o], along(o + 1))
        back.start()
        return back

    forwards = arrived(0)
    part = cross(0, forwards)
    forwards = arrived(1)
    backs = [send_back(0, part)]
    part = cross(1, forwards)
    for t in range(HALF):
        near_sib[t] = near[t, COLS:, :]
    near_copy = remote(near_sib, near_recv, s_nr, r_nr, sibling)
    near_copy.start()
    backs.append(send_back(1, part))

    for copy in x_copies:
        copy.wait()
    lane = lax.broadcasted_iota(jnp.int32, (COLS, 128), 1) // RANK
    for t in range(TOPS):
        for f in range(FAR):
            code = far_idx[t * FAR + f]
            tile = table[code >> 2].astype(F32)
            folded[t * FAR + f] = jnp.where(lane == (code & 3), tile, 0.0).astype(BF16)
    ones_row = lax.rem(lax.broadcasted_iota(jnp.int32, (128, 128), 0), RANK)
    ones_col = lax.rem(lax.broadcasted_iota(jnp.int32, (128, 128), 1), RANK)
    spread = jnp.where(ones_row == ones_col, 1.0, 0.0).astype(BF16)
    picked = []
    for t in range(TOPS):
        tiles = folded[t * FAR : (t + 1) * FAR].reshape(FAR * COLS, 128)
        everywhere = mm(tiles, spread)
        groups = []
        for g in range(FAR // 4):
            total = None
            for k in range(4):
                f = 4 * g + k
                term = jnp.where(lane == k, everywhere[f * COLS : (f + 1) * COLS], 0.0)
                total = term if total is None else total + term
            groups.append(total.astype(BF16))
        picked.append(jnp.concatenate(groups, axis=1))
    distant = mm_nt(jnp.concatenate(picked, axis=0), far_mat[...])
    for t in range(TOPS):
        far_top[t] = distant[t * COLS : (t + 1) * COLS, t * RANK : (t + 1) * RANK]
    for c in range(CL):
        lower = mm_nt(far_top[parent[c]], down[c], HIGHEST).astype(BF16)
        out[:, c * PS : (c + 1) * PS] = mm(lower, tgt_basis[c])

    near_copy.wait()
    for t in range(HALF):
        at = pl.ds(pl.multiple_of((mine + t) * PS, PS), PS)
        out[:, at] += near[t, 0:COLS, :]
        at = pl.ds(pl.multiple_of((other + t) * PS, PS), PS)
        out[:, at] += near_recv[t]
    for o in range(W):
        backs[o].wait()
        behind = jnp.where(me - o - 1 >= 0, 1.0, 0.0).astype(F32)
        for c in range(CL):
            at = pl.ds(c * PS, PS)
            given = ret_recv[o][ridx[o][RANKED + c]].astype(F32)
            keep = behind * ridx[o][PRESENT + c].astype(F32)
            out[:, at] += keep * given


def index_table(targets, sources):
    slots = jnp.arange(CL, dtype=jnp.int32)
    present = jnp.any(sources[None, :] == slots[:, None], axis=1).astype(jnp.int32)
    rank = jnp.sum(jnp.where(slots[None, :] < slots[:, None], present[None, :], 0), axis=1)
    place = (rank[None, :] == jnp.arange(CAP)[:, None]) & (present[None, :] == 1)
    listed = jnp.sum(jnp.where(place, slots[None, :], 0), axis=1)
    named = jnp.sum(
        jnp.where(targets[None, :] == slots[:, None], sources[None, :], 0), axis=1
    )
    slot = jnp.sum(jnp.where(named[:, None] == slots[None, :], rank[None, :], 0), axis=1)
    rank = jnp.minimum(rank, CAP - 1) * present
    pad = jnp.zeros((128 - 56,), jnp.int32)
    return jnp.concatenate([listed, slot, rank, present, pad]).astype(jnp.int32)


def local(
    centers,
    normals,
    weights,
    density,
    near_pairs,
    parent,
    far_src,
    src_basis,
    upward_transfer,
    far_mat,
    downward_transfer,
    tgt_basis,
):
    tables = [index_table(near_pairs[0, o], near_pairs[1, o]) for o in range(W)]
    dev, lane = far_src // TOPS, far_src % TOPS
    place = ((dev // (Y * Z)) * Y + dev % Y) * Z + (dev // Y) % Z
    far_idx = ((place * 2 + lane // 4) * 4 + lane % 4).reshape(-1).astype(jnp.int32)

    vmem = pl.BlockSpec(memory_space=pltpu.VMEM)
    smem = pl.BlockSpec(memory_space=pltpu.SMEM)
    dma = pltpu.SemaphoreType.DMA
    return pl.pallas_call(
        kernel,
        out_shape=jax.ShapeDtypeStruct((COLS, CL * PS), F32),
        in_specs=[vmem] * 4 + [smem] * 4 + [vmem] * 5,
        out_specs=vmem,
        scratch_shapes=[
            pltpu.VMEM((CL, 8, PS), F32),
            pltpu.VMEM((CL, COLS, PS), BF16),
            pltpu.VMEM((HALF, PS, 128), BF16),
            pltpu.VMEM((HALF, 80, PS), BF16),
            pltpu.VMEM((COLS, HALF * PS), BF16),
            pltpu.VMEM((W, CAP, COLS, PS), BF16),
            pltpu.VMEM((W, 2, 16, PS), BF16),
            pltpu.VMEM((CAP, COLS, PS), BF16),
            pltpu.VMEM((CAP, COLS, PS), BF16),
            pltpu.VMEM((CAP, COLS, PS), BF16),
            pltpu.VMEM((CAP, COLS, PS), BF16),
            pltpu.VMEM((4, 16, PS), BF16),
            pltpu.VMEM((4, 16, PS), BF16),
            pltpu.VMEM((CAP, 80, PS), BF16),
            pltpu.VMEM((HALF, 2 * COLS, PS), F32),
            pltpu.VMEM((HALF, 2 * COLS, PS), F32),
            pltpu.VMEM((W, CAP, COLS, PS), F32),
            pltpu.VMEM((W, CAP, COLS, PS), F32),
            pltpu.VMEM((W, CAP, COLS, PS), F32),
            pltpu.VMEM((W, CAP, COLS, PS), BF16),
            pltpu.VMEM((CAP, COLS, PS), BF16),
            pltpu.VMEM((CAP, COLS, PS), BF16),
            pltpu.VMEM((HALF, COLS, PS), F32),
            pltpu.VMEM((HALF, COLS, PS), F32),
            pltpu.VMEM((2 * N, COLS, 128), BF16),
            pltpu.VMEM((TOPS * FAR, COLS, 128), BF16),
            pltpu.VMEM((TOPS, COLS, RANK), F32),
            pltpu.SMEM((128,), jnp.int32),
            pltpu.SMEM((128,), jnp.int32),
            dma((W,)), dma((W,)),
            dma, dma,
            dma((W,)), dma((W,)),
            dma((W,)), dma((W,)),
            dma((W,)), dma((W,)),
            dma((W,)), dma((W,)),
            dma((W,)), dma((W,)),
            dma((W,)), dma((W,)),
            dma, dma,
            dma((Z - 1,)), dma((Z - 1,)),
            dma((Y - 1,)), dma((Y - 1,)),
            dma((X - 1,)), dma((X - 1,)),
        ],
        compiler_params=pltpu.CompilerParams(
            collective_id=0, has_side_effects=True, vmem_limit_bytes=56 * 1024 * 1024
        ),
    )(
        centers,
        normals,
        weights.reshape(1, -1),
        density,
        *tables,
        parent,
        far_idx,
        src_basis,
        upward_transfer,
        far_mat.reshape(TOPS * RANK, FAR * RANK),
        downward_transfer,
        tgt_basis,
    )


def solution(mesh):
    placed = (
        P(None, "clus"),
        P(None, "clus"),
        P("clus"),
        P("rhs", "clus"),
        P(None, None, "clus"),
        P("clus"),
        P("clus", None),
        P("clus", None, None),
        P("clus", None, None),
        P("clus", None, None),
        P("clus", None, None),
        P("clus", None, None),
    )
    return jax.shard_map(
        local, mesh=mesh, in_specs=placed, out_specs=P("rhs", "clus"), check_vma=False
    )
```

```python
import functools

import jax
import jax.numpy as jnp
from jax import lax
from jax.experimental import pallas as pl
from jax.experimental.pallas import tpu as pltpu
from jax.sharding import PartitionSpec as P

F32 = jnp.float32
BF16 = jnp.bfloat16
MESH = pl.DeviceIdType.MESH
HIGHEST = lax.Precision.HIGHEST

DELTA2 = 0.25
W = 2
X, Z, Y = 4, 8, 4
N = X * Z * Y
CL = 16
HALF = 8
CAP = 8
PS = 512
COLS = 16
RANK = 32
TOPS = 8
FAR = 32

LIST, RANKED, PRESENT = 0, 8, 24
POWER, LOG = 0, 16
PRIME = 19


def mm(a, b, precision=None):
    return jnp.dot(a, b, preferred_element_type=F32, precision=precision)


def mm_nt(a, b, precision=None):
    return lax.dot_general(
        a, b, (((1,), (1,)), ((), ())), preferred_element_type=F32, precision=precision
    )


def split3(v):
    high = v.astype(BF16).astype(F32)
    rest = v - high
    mid = rest.astype(BF16).astype(F32)
    return high, mid, rest - mid


def features(geo):
    row = lax.broadcasted_iota(jnp.int32, geo.shape, 0)
    low = row < 3
    mid = (row >= 3) & (row < 6)
    w = geo[6:7]
    weighted = geo * w
    xh = weighted.astype(BF16).astype(F32)
    xl = weighted - xh
    yh = jnp.where(low, jnp.roll(xh, -3, axis=0), 0.0)
    yl = jnp.where(low, jnp.roll(xl, -3, axis=0), 0.0)
    c0, c1, c2 = geo[0:1], geo[1:2], geo[2:3]
    square = c0 * c0 + c1 * c1 + c2 * c2 + 0.5 * DELTA2
    offset = -(weighted[3:4] * c0 + weighted[4:5] * c1 + weighted[5:6] * c2)

    def rows_3_to_5(parts, base):
        h, m, l = parts
        return jnp.where(row == 3, h, jnp.where(row == 4, m, jnp.where(row == 5, l, base)))

    sh, sm, sl = split3(square)
    q1 = [
        rows_3_to_5((sh, sm, sl), jnp.where(low, -2.0 * geo, 0.0)),
        jnp.where(low, 1.0, 0.0),
    ]
    q2 = [
        jnp.where(low, geo, jnp.where(mid, 1.0, 0.0)),
        jnp.where(row == 0, sh, jnp.where(row == 1, sm, jnp.where(row == 2, sl, 0.0))),
    ]
    u = [jnp.where(low, xh, jnp.where(mid, w, 0.0)), xl, xh, xl]
    v = [rows_3_to_5(split3(offset), yh), yh, yl, yl]
    return q1, q2, u, v


def target_features(geo):
    q1, q2, u, v = features(geo)
    pad = jnp.zeros((48, PS), F32)
    left = jnp.concatenate(q1 + u + v + [pad], axis=0).T.astype(BF16)
    return left, jnp.concatenate(q2 + v + u, axis=0).astype(BF16)


def source_features(geo):
    q1, q2, u, v = features(geo)
    return jnp.concatenate(q2 + v + u, axis=0).astype(BF16)


def cube(q):
    t = lax.rsqrt(q)
    return t * t * t


def name_sources(pairs, o, small, idx):
    named = 0
    for p in range(CL):
        named = named | small[POWER + pairs[1, o, p]]
    before = 0
    for c in range(CL):
        present = (named >> c) & 1
        idx[RANKED + c] = before * present
        idx[PRESENT + c] = present
        before = before + present
    for m in range(CAP):
        lowest = named & (-named)
        idx[LIST + m] = small[LOG + lax.rem(lowest, PRIME)]
        named = named - lowest


def name_targets(pairs, o, mine, idx, slots):
    for t in range(HALF):
        source = 0
        for p in range(CL):
            source = source + jnp.where(pairs[0, o, p] == mine + t, pairs[1, o, p], 0)
        slots[t] = idx[RANKED + source]


def kernel(
    cen, nor, wts, den, pairs, parent, far_src, src_basis_hbm, up_hbm, far_mat_hbm, down_hbm,
    tgt_basis_hbm,
    out,
    src_basis, up, far_mat, down, tgt_basis, s_in,
    small, geo, dens, left, right, dsib, sendd, sendg, bown1, bown2, bsib1, bsib2, bgeo1, bgeo2,
    bright, near, ybuf, fbuf, part_own, part_sib, part_recv, ret_send, ret_recv1, ret_recv2,
    near_sib, near_recv, table, folded, far_top, idx1, idx2, ridx1, ridx2, slots1, slots2,
    s_idx, r_idx, s_sib, r_sib, s_bd, r_bd, s_bg, r_bg, s_fd, r_fd, s_fg, r_fg, s_ps, r_ps,
    s_rt, r_rt, s_nr, r_nr, s_z, r_z, s_y, r_y, s_x, r_x,
):
    me = lax.axis_index("clus")
    core = lax.axis_index("rhs")
    y = lax.rem(me, Y)
    z = lax.rem(me // Y, Z)
    x = me // (Y * Z)
    idx = (idx1, idx2)
    ridx = (ridx1, ridx2)
    slots = (slots1, slots2)
    bown, bsib, bgeo = (bown1, bown2), (bsib1, bsib2), (bgeo1, bgeo2)
    ret_recv = (ret_recv1, ret_recv2)
    mine = core * HALF
    other = (1 - core) * HALF

    def along(step):
        return {"clus": lax.rem(me + step + N, N)}

    sibling = {"rhs": 1 - core}
    z_peers = [{"clus": (x * Z + lax.rem(z + k, Z)) * Y + y} for k in range(1, Z)]
    y_peers = [{"clus": (x * Z + z) * Y + lax.rem(y + k, Y)} for k in range(1, Y)]
    x_peers = [{"clus": (lax.rem(x + k, X) * Z + z) * Y + y} for k in range(1, X)]

    def remote(src, dst, send, recv, to):
        return pltpu.make_async_remote_copy(
            src_ref=src, dst_ref=dst, send_sem=send, recv_sem=recv, device_id=to, device_id_type=MESH
        )

    barrier = pltpu.get_barrier_semaphore()
    partners = [sibling] + [along(s) for s in (1, 2, -1, -2)] + z_peers + y_peers + x_peers
    for partner in partners:
        pl.semaphore_signal(barrier, inc=1, device_id=partner, device_id_type=MESH)
    loads = [
        pltpu.make_async_copy(src, dst, s_in.at[k])
        for k, (src, dst) in enumerate(
            (
                (src_basis_hbm, src_basis),
                (up_hbm, up),
                (far_mat_hbm, far_mat),
                (down_hbm, down),
                (tgt_basis_hbm, tgt_basis),
            )
        )
    ]
    for load in loads:
        load.start()
    for c in range(CL):
        small[POWER + c] = 1 << c
    for p in range(PRIME):
        small[LOG + p] = 0
    for c in range(CL):
        small[LOG + (1 << c) % PRIME] = c
    for o in range(W):
        name_sources(pairs, o, small, idx[o])
    pl.semaphore_wait(barrier, len(partners))

    idx_copies = [
        remote(idx[o], ridx[o], s_idx.at[o], r_idx.at[o], along(o + 1)) for o in range(W)
    ]
    for copy in idx_copies:
        copy.start()
    sib_copy = remote(
        den.at[:, pl.ds(pl.multiple_of(other * PS, PS), HALF * PS)], dsib, s_sib, r_sib, sibling
    )
    sib_copy.start()

    for c in range(CL):
        at = pl.ds(c * PS, PS)
        rows = [cen[:, at].astype(F32), nor[:, at].astype(F32), wts[:, at].astype(F32)]
        dens[c] = den[:, at]
        geo[c] = jnp.concatenate(rows + [jnp.zeros((1, PS), F32)], axis=0)

    loads[0].wait()
    loads[1].wait()
    tops = [jnp.zeros((COLS, RANK), F32) for _ in range(TOPS)]
    for c in range(CL):
        leaf = mm_nt(den[:, c * PS : (c + 1) * PS], src_basis[c])
        child = mm_nt(leaf, up[c], HIGHEST)
        for t in range(TOPS):
            tops[t] = tops[t] + jnp.where(parent[c] == t, child, 0.0)
    for h in range(2):
        table[2 * me + h] = jnp.concatenate(tops[4 * h : 4 * h + 4], axis=1).astype(BF16)

    def gather_step(start, size, peers, send, recv):
        block = table.at[pl.ds(start, size)]
        copies = [
            remote(block, block, send.at[k], recv.at[k], to) for k, to in enumerate(peers)
        ]
        for copy in copies:
            copy.start()
        return copies

    y_copies = gather_step(2 * me, 2, y_peers, s_y, r_y)

    b_copies = []
    for o in range(W):
        idx_copies[o].wait()
        for m in range(CAP):
            sendd[o, m] = dens[ridx[o][LIST + m]]
        for m in range(2):
            c0 = ridx[o][LIST + core * 4 + 2 * m]
            c1 = ridx[o][LIST + core * 4 + 2 * m + 1]
            sendg[o, m] = jnp.concatenate([geo[c0], geo[c1]], axis=0).astype(BF16)
        half = pl.ds(core * 2, 2)
        copies = (
            remote(sendg.at[o], bgeo[o].at[half], s_bg.at[o], r_bg.at[o], along(-o - 1)),
            remote(sendd.at[o], bown[o], s_bd.at[o], r_bd.at[o], along(-o - 1)),
        )
        b_copies.append(copies)
        if o == 0:
            for copy in copies:
                copy.start()

    for t in range(HALF):
        left[t], right[t] = target_features(geo[mine + t])
    for copy in b_copies[1]:
        copy.start()
    for copy in y_copies:
        copy.wait()
    z_copies = gather_step((x * Z + z) * Y * 2, Y * 2, z_peers, s_z, r_z)
    sib_copy.wait()
    for o in range(W):
        name_targets(pairs, o, mine, idx[o], slots[o])

    def densities(t):
        own = den[:, pl.ds(pl.multiple_of((mine + t) * PS, PS), PS)]
        return jnp.concatenate([own, dsib[:, pl.ds(pl.multiple_of(t * PS, PS), PS)]], axis=0)

    def self_pair(u, carry):
        for k in range(2):
            t = 2 * u + k
            q = mm(left[t, :, 0:16], right[t, 0:16])
            nb = mm(left[t, :, 48:80], right[t, 48:80])
            near[t] = mm(densities(t), (nb * cube(q)).astype(BF16))
        return carry

    lax.fori_loop(0, HALF // 2, self_pair, 0)

    for copy in z_copies:
        copy.wait()
    x_copies = gather_step(x * Y * Z * 2, Y * Z * 2, x_peers, s_x, r_x)

    def arrived(o):
        for copy in b_copies[o]:
            copy.wait()
        half = pl.ds(core * 2, 2)
        forwards = (
            remote(bgeo[o].at[half], bgeo[o].at[half], s_fg.at[o], r_fg.at[o], sibling),
            remote(bown[o], bsib[o], s_fd.at[o], r_fd.at[o], sibling),
        )
        for copy in forwards:
            copy.start()
        return forwards

    def prepare(o, forwards):
        for copy in forwards:
            copy.wait()
        for m in range(CAP):
            pair = bgeo[o][m // 2].astype(F32)
            bright[m] = source_features(pair[8 * (m % 2) : 8 * (m % 2) + 8])

    def cross(o, first, last, later):
        def cross_pair(u, carry):
            for k in range(2):
                t = 2 * u + k
                m = slots[o][t]
                q = mm(left[t, :, 0:16], bright[m, 0:16])
                nf = mm(left[t, :, 16:48], bright[m, 16:48])
                nb = mm(left[t, :, 48:80], bright[m, 48:80])
                scale = cube(q)
                ybuf[t] = mm(densities(t), (nb * scale).astype(BF16))
                if later:
                    fbuf[t] = (nf * scale).astype(BF16)
                else:
                    there = jnp.concatenate([bown[o][m], bsib[o][m]], axis=0)
                    near[t] += live(o) * mm_nt(there, (nf * scale).astype(BF16))
            return carry

        lax.fori_loop(first // 2, last // 2, cross_pair, 0)

    def live(o):
        return jnp.where(me + o + 1 < N, 1.0, 0.0).astype(F32)

    def cross_rest(o):
        def rest_pair(u, carry):
            for k in range(2):
                t = 2 * u + k
                m = slots[o][t]
                there = jnp.concatenate([bown[o][m], bsib[o][m]], axis=0)
                near[t] += live(o) * mm_nt(there, fbuf[t])
            return carry

        lax.fori_loop(0, HALF // 2, rest_pair, 0)

    def share(o):
        copy = None
        for rows, dst in ((COLS, part_sib), (0, part_own)):
            for r in range(0, COLS, 8):
                tiles = [ybuf[t, rows + r : rows + r + 8, :] for t in range(HALF)]
                for m in range(CAP):
                    total = None
                    for t in range(HALF):
                        hit = jnp.where(slots[o][t] == m, 1.0, 0.0).astype(F32)
                        term = hit * tiles[t]
                        total = term if total is None else total + term
                    dst[o, m, r : r + 8, :] = total
            if copy is None:
                copy = remote(part_sib.at[o], part_recv.at[o], s_ps.at[o], r_ps.at[o], sibling)
                copy.start()
        return copy

    def send_back(o, copy):
        copy.wait()
        for m in range(CAP):
            ret_send[o, m] = (part_own[o, m] + part_recv[o, m]).astype(BF16)
        back = remote(ret_send.at[o], ret_recv[o], s_rt.at[o], r_rt.at[o], along(o + 1))
        back.start()
        return back

    prepare(0, arrived(0))
    cross(0, 0, 4, False)
    forwards = arrived(1)
    cross(0, 4, 8, False)
    part = share(0)
    prepare(1, forwards)
    cross(1, 0, 4, True)
    backs = [send_back(0, part)]
    cross(1, 4, 8, True)
    part = share(1)
    cross_rest(1)
    backs.append(send_back(1, part))
    for t in range(HALF):
        near_sib[t] = near[t, COLS:, :]
    near_copy = remote(near_sib, near_recv, s_nr, r_nr, sibling)
    near_copy.start()

    for load in loads[2:]:
        load.wait()
    for copy in x_copies:
        copy.wait()
    lane = lax.broadcasted_iota(jnp.int32, (COLS, 128), 1) // RANK
    for t in range(TOPS):
        for f in range(FAR):
            top = far_src[t, f]
            tile = table[top >> 2].astype(F32)
            folded[t * FAR + f] = jnp.where(lane == (top & 3), tile, 0.0).astype(BF16)
    ones_row = lax.rem(lax.broadcasted_iota(jnp.int32, (128, 128), 0), RANK)
    ones_col = lax.rem(lax.broadcasted_iota(jnp.int32, (128, 128), 1), RANK)
    spread = jnp.where(ones_row == ones_col, 1.0, 0.0).astype(BF16)
    picked = []
    for t in range(TOPS):
        tiles = folded[t * FAR : (t + 1) * FAR].reshape(FAR * COLS, 128)
        everywhere = mm(tiles, spread)
        groups = []
        for g in range(FAR // 4):
            total = None
            for k in range(4):
                f = 4 * g + k
                term = jnp.where(lane == k, everywhere[f * COLS : (f + 1) * COLS], 0.0)
                total = term if total is None else total + term
            groups.append(total.astype(BF16))
        picked.append(jnp.concatenate(groups, axis=1))
    distant = mm_nt(jnp.concatenate(picked, axis=0), far_mat[...])
    for t in range(TOPS):
        far_top[t] = distant[t * COLS : (t + 1) * COLS, t * RANK : (t + 1) * RANK]
    for c in range(CL):
        lower = mm_nt(far_top[parent[c]], down[c], HIGHEST).astype(BF16)
        out[:, c * PS : (c + 1) * PS] = mm(lower, tgt_basis[c])

    near_copy.wait()
    for t in range(HALF):
        at = pl.ds(pl.multiple_of((mine + t) * PS, PS), PS)
        out[:, at] += near[t, 0:COLS, :]
        at = pl.ds(pl.multiple_of((other + t) * PS, PS), PS)
        out[:, at] += near_recv[t]
    for o in range(W):
        backs[o].wait()
        behind = jnp.where(me - o - 1 >= 0, 1.0, 0.0).astype(F32)
        for c in range(CL):
            at = pl.ds(c * PS, PS)
            given = ret_recv[o][ridx[o][RANKED + c]].astype(F32)
            keep = behind * ridx[o][PRESENT + c].astype(F32)
            out[:, at] += keep * given


def local(
    centers,
    normals,
    weights,
    density,
    near_pairs,
    parent,
    far_src,
    src_basis,
    upward_transfer,
    far_mat,
    downward_transfer,
    tgt_basis,
):
    vmem = pl.BlockSpec(memory_space=pltpu.VMEM)
    smem = pl.BlockSpec(memory_space=pltpu.SMEM)
    dma = pltpu.SemaphoreType.DMA
    return pl.pallas_call(
        kernel,
        out_shape=jax.ShapeDtypeStruct((COLS, CL * PS), F32),
        in_specs=[vmem] * 4 + [smem] * 3 + [pl.BlockSpec(memory_space=pl.ANY)] * 5,
        out_specs=vmem,
        scratch_shapes=[
            pltpu.VMEM((CL, RANK, PS), BF16),
            pltpu.VMEM((CL, RANK, RANK), F32),
            pltpu.VMEM((TOPS * RANK, FAR * RANK), BF16),
            pltpu.VMEM((CL, RANK, RANK), F32),
            pltpu.VMEM((CL, RANK, PS), BF16),
            dma((5,)),
            pltpu.SMEM((64,), jnp.int32),
            pltpu.VMEM((CL, 8, PS), F32),
            pltpu.VMEM((CL, COLS, PS), BF16),
            pltpu.VMEM((HALF, PS, 128), BF16),
            pltpu.VMEM((HALF, 80, PS), BF16),
            pltpu.VMEM((COLS, HALF * PS), BF16),
            pltpu.VMEM((W, CAP, COLS, PS), BF16),
            pltpu.VMEM((W, 2, 16, PS), BF16),
            pltpu.VMEM((CAP, COLS, PS), BF16),
            pltpu.VMEM((CAP, COLS, PS), BF16),
            pltpu.VMEM((CAP, COLS, PS), BF16),
            pltpu.VMEM((CAP, COLS, PS), BF16),
            pltpu.VMEM((4, 16, PS), BF16),
            pltpu.VMEM((4, 16, PS), BF16),
            pltpu.VMEM((CAP, 80, PS), BF16),
            pltpu.VMEM((HALF, 2 * COLS, PS), F32),
            pltpu.VMEM((HALF, 2 * COLS, PS), F32),
            pltpu.VMEM((HALF, PS, PS), BF16),
            pltpu.VMEM((W, CAP, COLS, PS), F32),
            pltpu.VMEM((W, CAP, COLS, PS), F32),
            pltpu.VMEM((W, CAP, COLS, PS), F32),
            pltpu.VMEM((W, CAP, COLS, PS), BF16),
            pltpu.VMEM((CAP, COLS, PS), BF16),
            pltpu.VMEM((CAP, COLS, PS), BF16),
            pltpu.VMEM((HALF, COLS, PS), F32),
            pltpu.VMEM((HALF, COLS, PS), F32),
            pltpu.VMEM((2 * N, COLS, 128), BF16),
            pltpu.VMEM((TOPS * FAR, COLS, 128), BF16),
            pltpu.VMEM((TOPS, COLS, RANK), F32),
            pltpu.SMEM((128,), jnp.int32),
            pltpu.SMEM((128,), jnp.int32),
            pltpu.SMEM((128,), jnp.int32),
            pltpu.SMEM((128,), jnp.int32),
            pltpu.SMEM((HALF,), jnp.int32),
            pltpu.SMEM((HALF,), jnp.int32),
            dma((W,)), dma((W,)),
            dma, dma,
            dma((W,)), dma((W,)),
            dma((W,)), dma((W,)),
            dma((W,)), dma((W,)),
            dma((W,)), dma((W,)),
            dma((W,)), dma((W,)),
            dma((W,)), dma((W,)),
            dma, dma,
            dma((Z - 1,)), dma((Z - 1,)),
            dma((Y - 1,)), dma((Y - 1,)),
            dma((X - 1,)), dma((X - 1,)),
        ],
        compiler_params=pltpu.CompilerParams(
            collective_id=0, has_side_effects=True, vmem_limit_bytes=56 * 1024 * 1024
        ),
    )(
        centers,
        normals,
        weights.reshape(1, -1),
        density,
        near_pairs,
        parent,
        far_src,
        src_basis,
        upward_transfer,
        far_mat.reshape(TOPS * RANK, FAR * RANK),
        downward_transfer,
        tgt_basis,
    )


def solution(mesh):
    placed = (
        P(None, "clus"),
        P(None, "clus"),
        P("clus"),
        P("rhs", "clus"),
        P(None, None, "clus"),
        P("clus"),
        P("clus", None),
        P("clus", None, None),
        P("clus", None, None),
        P("clus", None, None),
        P("clus", None, None),
        P("clus", None, None),
    )
    return jax.shard_map(
        local, mesh=mesh, in_specs=placed, out_specs=P("rhs", "clus"), check_vma=False
    )
```

```python
import functools

import jax
import jax.numpy as jnp
from jax import lax
from jax.experimental import pallas as pl
from jax.experimental.pallas import tpu as pltpu
from jax.sharding import PartitionSpec as P

F32 = jnp.float32
BF16 = jnp.bfloat16
MESH = pl.DeviceIdType.MESH
HIGHEST = lax.Precision.HIGHEST

DELTA2 = 0.25
W = 2
X, Z, Y = 4, 8, 4
N = X * Z * Y
CL = 16
HALF = 8
CAP = 8
PS = 512
COLS = 16
RANK = 32
TOPS = 8
FAR = 32

LIST, RANKED, PRESENT = 0, 8, 24
POWER, LOG = 0, 16
PRIME = 19


def mm(a, b, precision=None):
    return jnp.dot(a, b, preferred_element_type=F32, precision=precision)


def mm_nt(a, b, precision=None):
    return lax.dot_general(
        a, b, (((1,), (1,)), ((), ())), preferred_element_type=F32, precision=precision
    )


def split3(v):
    high = v.astype(BF16).astype(F32)
    rest = v - high
    mid = rest.astype(BF16).astype(F32)
    return high, mid, rest - mid


def features(geo):
    row = lax.broadcasted_iota(jnp.int32, geo.shape, 0)
    low = row < 3
    mid = (row >= 3) & (row < 6)
    w = geo[6:7]
    weighted = geo * w
    xh = weighted.astype(BF16).astype(F32)
    xl = weighted - xh
    yh = jnp.where(low, jnp.roll(xh, -3, axis=0), 0.0)
    yl = jnp.where(low, jnp.roll(xl, -3, axis=0), 0.0)
    c0, c1, c2 = geo[0:1], geo[1:2], geo[2:3]
    square = c0 * c0 + c1 * c1 + c2 * c2 + 0.5 * DELTA2
    offset = -(weighted[3:4] * c0 + weighted[4:5] * c1 + weighted[5:6] * c2)

    def rows_3_to_5(parts, base):
        h, m, l = parts
        return jnp.where(row == 3, h, jnp.where(row == 4, m, jnp.where(row == 5, l, base)))

    sh, sm, sl = split3(square)
    q1 = [
        rows_3_to_5((sh, sm, sl), jnp.where(low, -2.0 * geo, 0.0)),
        jnp.where(low, 1.0, 0.0),
    ]
    q2 = [
        jnp.where(low, geo, jnp.where(mid, 1.0, 0.0)),
        jnp.where(row == 0, sh, jnp.where(row == 1, sm, jnp.where(row == 2, sl, 0.0))),
    ]
    u = [jnp.where(low, xh, jnp.where(mid, w, 0.0)), xl, xh, xl]
    v = [rows_3_to_5(split3(offset), yh), yh, yl, yl]
    return q1, q2, u, v


def target_features(geo):
    q1, q2, u, v = features(geo)
    pad = jnp.zeros((48, PS), F32)
    left = jnp.concatenate(q1 + u + v + [pad], axis=0).T.astype(BF16)
    return left, jnp.concatenate(q2 + v + u, axis=0).astype(BF16)


def source_features(geo):
    q1, q2, u, v = features(geo)
    return jnp.concatenate(q2 + v + u, axis=0).astype(BF16)


def cube(q):
    t = lax.rsqrt(q)
    return t * t * t


def name_sources(pairs, o, small, idx):
    named = 0
    for p in range(CL):
        named = named | small[POWER + pairs[1, o, p]]
    before = 0
    for c in range(CL):
        present = (named >> c) & 1
        idx[RANKED + c] = before * present
        idx[PRESENT + c] = present
        before = before + present
    for m in range(CAP):
        lowest = named & (-named)
        idx[LIST + m] = small[LOG + lax.rem(lowest, PRIME)]
        named = named - lowest


def name_targets(pairs, o, mine, idx, slots):
    for t in range(HALF):
        source = 0
        for p in range(CL):
            source = source + jnp.where(pairs[0, o, p] == mine + t, pairs[1, o, p], 0)
        slots[t] = idx[RANKED + source]


def kernel(
    cen, nor, wts, den, pairs, parent, far_src, src_basis_hbm, up_hbm, far_mat_hbm, down_hbm,
    tgt_basis_hbm,
    out,
    src_basis, up, far_mat, down, tgt_basis, s_in,
    small, geo, dens, left, right, dsib, sendd, sendg, bown1, bown2, bsib1, bsib2, bgeo1, bgeo2,
    bright, near, ybuf, fbuf, part_own, part_sib, part_recv, ret_send, ret_recv1, ret_recv2,
    near_sib, near_recv, table, folded, far_top, idx1, idx2, ridx1, ridx2, slots1, slots2,
    s_idx, r_idx, s_sib, r_sib, s_bd, r_bd, s_bg, r_bg, s_fd, r_fd, s_fg, r_fg, s_ps, r_ps,
    s_rt, r_rt, s_nr, r_nr, s_z, r_z, s_y, r_y, s_x, r_x,
):
    me = lax.axis_index("clus")
    core = lax.axis_index("rhs")
    y = lax.rem(me, Y)
    z = lax.rem(me // Y, Z)
    x = me // (Y * Z)
    idx = (idx1, idx2)
    ridx = (ridx1, ridx2)
    slots = (slots1, slots2)
    bown, bsib, bgeo = (bown1, bown2), (bsib1, bsib2), (bgeo1, bgeo2)
    ret_recv = (ret_recv1, ret_recv2)
    mine = core * HALF
    other = (1 - core) * HALF

    ahead = [me + o + 1 < N for o in range(W)]
    behind = [me - o - 1 >= 0 for o in range(W)]

    def when(condition, *steps):
        @pl.when(condition)
        def _():
            for step in steps:
                step()

    def along(step):
        return {"clus": lax.rem(me + step + N, N)}

    sibling = {"rhs": 1 - core}
    z_peers = [{"clus": (x * Z + lax.rem(z + k, Z)) * Y + y} for k in range(1, Z)]
    y_peers = [{"clus": (x * Z + z) * Y + lax.rem(y + k, Y)} for k in range(1, Y)]
    x_peers = [{"clus": (lax.rem(x + k, X) * Z + z) * Y + y} for k in range(1, X)]

    def remote(src, dst, send, recv, to):
        return pltpu.make_async_remote_copy(
            src_ref=src, dst_ref=dst, send_sem=send, recv_sem=recv, device_id=to, device_id_type=MESH
        )

    barrier = pltpu.get_barrier_semaphore()
    partners = [sibling] + [along(s) for s in (1, 2, -1, -2)] + z_peers + y_peers + x_peers
    for partner in partners:
        pl.semaphore_signal(barrier, inc=1, device_id=partner, device_id_type=MESH)
    loads = [
        pltpu.make_async_copy(src, dst, s_in.at[k])
        for k, (src, dst) in enumerate(
            (
                (src_basis_hbm, src_basis),
                (up_hbm, up),
                (far_mat_hbm, far_mat),
                (down_hbm, down),
                (tgt_basis_hbm, tgt_basis),
            )
        )
    ]
    for load in loads:
        load.start()
    for c in range(CL):
        small[POWER + c] = 1 << c
    for p in range(PRIME):
        small[LOG + p] = 0
    for c in range(CL):
        small[LOG + (1 << c) % PRIME] = c
    for o in range(W):
        name_sources(pairs, o, small, idx[o])
    pl.semaphore_wait(barrier, len(partners))

    idx_copies = [
        remote(idx[o], ridx[o], s_idx.at[o], r_idx.at[o], along(o + 1)) for o in range(W)
    ]
    for o in range(W):
        when(ahead[o], idx_copies[o].start)
    sib_copy = remote(
        den.at[:, pl.ds(pl.multiple_of(other * PS, PS), HALF * PS)], dsib, s_sib, r_sib, sibling
    )
    sib_copy.start()

    for c in range(CL):
        at = pl.ds(c * PS, PS)
        w = wts[at].astype(F32).reshape(1, PS)
        rows = [cen[:, at].astype(F32), nor[:, at].astype(F32), w]
        dens[c] = den[:, at]
        geo[c] = jnp.concatenate(rows + [jnp.zeros((1, PS), F32)], axis=0)

    loads[0].wait()
    loads[1].wait()
    def blocks(wide):
        return [
            wide[c * COLS : (c + 1) * COLS, c * RANK : (c + 1) * RANK] for c in range(CL)
        ]

    leaf = mm_nt(dens[...].reshape(CL * COLS, PS), src_basis[...].reshape(CL * RANK, PS))
    leaf = jnp.concatenate(blocks(leaf), axis=0)
    tops = [jnp.zeros((COLS, RANK), F32) for _ in range(TOPS)]
    for c, child in enumerate(blocks(mm_nt(leaf, up[...].reshape(CL * RANK, RANK), HIGHEST))):
        for t in range(TOPS):
            tops[t] = tops[t] + jnp.where(parent[c] == t, child, 0.0)
    for h in range(2):
        table[2 * me + h] = jnp.concatenate(tops[4 * h : 4 * h + 4], axis=1).astype(BF16)

    def gather_step(start, size, peers, send, recv):
        block = table.at[pl.ds(start, size)]
        copies = [
            remote(block, block, send.at[k], recv.at[k], to) for k, to in enumerate(peers)
        ]
        for copy in copies:
            copy.start()
        return copies

    y_copies = gather_step(2 * me, 2, y_peers, s_y, r_y)

    b_copies = []
    for o in range(W):

        def gather(o=o):
            idx_copies[o].wait_recv()
            for m in range(CAP):
                sendd[o, m] = dens[ridx[o][LIST + m]]
            for m in range(2):
                c0 = ridx[o][LIST + core * 4 + 2 * m]
                c1 = ridx[o][LIST + core * 4 + 2 * m + 1]
                sendg[o, m] = jnp.concatenate([geo[c0], geo[c1]], axis=0).astype(BF16)

        when(behind[o], gather)
        half = pl.ds(core * 2, 2)
        copies = (
            remote(sendg.at[o], bgeo[o].at[half], s_bg.at[o], r_bg.at[o], along(-o - 1)),
            *(
                remote(
                    sendd.at[o, pl.ds(4 * h, 4)], bown[o].at[pl.ds(4 * h, 4)],
                    s_bd.at[o, h], r_bd.at[o, h], along(-o - 1),
                )
                for h in range(2)
            ),
        )
        b_copies.append(copies)
        if o == 0:
            when(behind[o], *(copy.start for copy in copies))

    for t in range(HALF):
        left[t], right[t] = target_features(geo[mine + t])
    for copy in y_copies:
        copy.wait()
    z_copies = gather_step((x * Z + z) * Y * 2, Y * 2, z_peers, s_z, r_z)
    sib_copy.wait()
    for o in range(W):
        name_targets(pairs, o, mine, idx[o], slots[o])

    def densities(t):
        own = den[:, pl.ds(pl.multiple_of((mine + t) * PS, PS), PS)]
        return jnp.concatenate([own, dsib[:, pl.ds(pl.multiple_of(t * PS, PS), PS)]], axis=0)

    def self_pair(u, carry):
        for k in range(2):
            t = 2 * u + k
            q = mm(left[t, :, 0:16], right[t, 0:16])
            nb = mm(left[t, :, 48:80], right[t, 48:80])
            near[t] = mm(densities(t), (nb * cube(q)).astype(BF16))
        return carry

    lax.fori_loop(0, HALF // 4, self_pair, 0)

    when(behind[1], *(copy.start for copy in b_copies[1]))
    for copy in z_copies:
        copy.wait()
    x_copies = gather_step(x * Y * Z * 2, Y * Z * 2, x_peers, s_x, r_x)

    def arrived(o):
        half = pl.ds(core * 2, 2)
        forwards = [remote(bgeo[o].at[half], bgeo[o].at[half], s_fg.at[o], r_fg.at[o], sibling)]
        for h in range(2):
            part = pl.ds(4 * h, 4)
            forwards.append(
                remote(bown[o].at[part], bsib[o].at[part], s_fd.at[o, h], r_fd.at[o, h], sibling)
            )

        def pass_on():
            for arrival, forward in zip(b_copies[o], forwards):
                arrival.wait_recv()
                forward.start()

        when(ahead[o], pass_on)
        when(behind[o], *(copy.wait_send for copy in b_copies[o]))
        return forwards

    def prepare(o, forwards):
        when(ahead[o], *(copy.wait for copy in forwards))
        for m in range(CAP):
            pair = bgeo[o][m // 2].astype(F32)
            bright[m] = source_features(pair[8 * (m % 2) : 8 * (m % 2) + 8])

    def cross(o, first, last, later):
        def cross_pair(u, carry):
            for k in range(2):
                t = 2 * u + k
                m = slots[o][t]
                q = mm(left[t, :, 0:16], bright[m, 0:16])
                nf = mm(left[t, :, 16:48], bright[m, 16:48])
                nb = mm(left[t, :, 48:80], bright[m, 48:80])
                scale = cube(q)
                ybuf[t] = mm(densities(t), (nb * scale).astype(BF16))
                if later:
                    fbuf[t] = (nf * scale).astype(BF16)
                else:
                    there = jnp.concatenate([bown[o][m], bsib[o][m]], axis=0)
                    there = mm_nt(there, (nf * scale).astype(BF16))
                    near[t] += jnp.where(ahead[o], there, 0.0)
            return carry

        lax.fori_loop(first // 2, last // 2, cross_pair, 0)

    def cross_rest(o):
        def rest_pair(u, carry):
            for k in range(2):
                t = 2 * u + k
                m = slots[o][t]
                there = jnp.concatenate([bown[o][m], bsib[o][m]], axis=0)
                near[t] += jnp.where(ahead[o], mm_nt(there, fbuf[t]), 0.0)
            return carry

        lax.fori_loop(0, HALF // 2, rest_pair, 0)

    def share(o):
        copies = []
        for h in range(2):
            for rows, dst in ((COLS, part_sib), (0, part_own)):
                for r in range(0, COLS, 8):
                    tiles = [ybuf[t, rows + r : rows + r + 8, :] for t in range(HALF)]
                    for m in range(4 * h, 4 * h + 4):
                        total = None
                        for t in range(HALF):
                            hit = jnp.where(slots[o][t] == m, 1.0, 0.0).astype(F32)
                            term = hit * tiles[t]
                            total = term if total is None else total + term
                        dst[o, m, r : r + 8, :] = total
                if rows == COLS:
                    part = pl.ds(4 * h, 4)
                    copies.append(
                        remote(
                            part_sib.at[o, part], part_recv.at[o, part],
                            s_ps.at[o, h], r_ps.at[o, h], sibling,
                        )
                    )
                    copies[-1].start()
        return copies

    def send_back(o, copies):
        returned = []
        for h in range(2):
            copies[h].wait()
            for m in range(4 * h, 4 * h + 4):
                ret_send[o, m] = (part_own[o, m] + part_recv[o, m]).astype(BF16)
            part = pl.ds(4 * h, 4)
            returned.append(
                remote(
                    ret_send.at[o, part], ret_recv[o].at[part],
                    s_rt.at[o, h], r_rt.at[o, h], along(o + 1),
                )
            )
            when(ahead[o], returned[-1].start)
        return returned

    forwards = arrived(0)
    lax.fori_loop(HALF // 4, HALF // 2, self_pair, 0)
    prepare(0, forwards)
    cross(0, 0, 4, False)
    forwards = arrived(1)
    cross(0, 4, 8, False)
    part = share(0)
    prepare(1, forwards)
    cross(1, 0, 4, True)
    backs = [send_back(0, part)]
    cross(1, 4, 8, True)
    part = share(1)
    cross_rest(1)
    backs.append(send_back(1, part))
    for t in range(HALF):
        near_sib[t] = near[t, COLS:, :]
    near_copy = remote(near_sib, near_recv, s_nr, r_nr, sibling)
    near_copy.start()

    for load in loads[2:]:
        load.wait()
    for copy in x_copies:
        copy.wait()
    lane = lax.broadcasted_iota(jnp.int32, (COLS, 128), 1) // RANK
    for t in range(TOPS):
        for f in range(FAR):
            top = far_src[t, f]
            tile = table[top >> 2].astype(F32)
            folded[t * FAR + f] = jnp.where(lane == (top & 3), tile, 0.0).astype(BF16)
    ones_row = lax.rem(lax.broadcasted_iota(jnp.int32, (128, 128), 0), RANK)
    ones_col = lax.rem(lax.broadcasted_iota(jnp.int32, (128, 128), 1), RANK)
    spread = jnp.where(ones_row == ones_col, 1.0, 0.0).astype(BF16)
    picked = []
    for t in range(TOPS):
        tiles = folded[t * FAR : (t + 1) * FAR].reshape(FAR * COLS, 128)
        everywhere = mm(tiles, spread)
        groups = []
        for g in range(FAR // 4):
            total = None
            for k in range(4):
                f = 4 * g + k
                term = jnp.where(lane == k, everywhere[f * COLS : (f + 1) * COLS], 0.0)
                total = term if total is None else total + term
            groups.append(total.astype(BF16))
        picked.append(jnp.concatenate(groups, axis=1))
    distant = mm_nt(jnp.concatenate(picked, axis=0), far_mat[...])
    for t in range(TOPS):
        far_top[t] = distant[t * COLS : (t + 1) * COLS, t * RANK : (t + 1) * RANK]
    upper = jnp.concatenate([far_top[parent[c]] for c in range(CL)], axis=0)
    lower = mm_nt(upper, down[...].reshape(CL * RANK, RANK), HIGHEST)
    same = lax.broadcasted_iota(jnp.int32, lower.shape, 0) // COLS == (
        lax.broadcasted_iota(jnp.int32, lower.shape, 1) // RANK
    )
    lower = jnp.where(same, lower, 0.0).astype(BF16)
    far_part = mm(lower, tgt_basis[...].reshape(CL * RANK, PS))
    for c in range(CL):
        out[:, c * PS : (c + 1) * PS] = far_part[c * COLS : (c + 1) * COLS]

    near_copy.wait()
    for t in range(HALF):
        at = pl.ds(pl.multiple_of((mine + t) * PS, PS), PS)
        out[:, at] += near[t, 0:COLS, :]
        at = pl.ds(pl.multiple_of((other + t) * PS, PS), PS)
        out[:, at] += near_recv[t]
    for o in range(W):
        when(ahead[o], idx_copies[o].wait_send, *(copy.wait_send for copy in backs[o]))

        def add(o=o):
            for copy in backs[o]:
                copy.wait_recv()
            for c in range(CL):
                at = pl.ds(c * PS, PS)
                given = ret_recv[o][ridx[o][RANKED + c]].astype(F32)
                out[:, at] += ridx[o][PRESENT + c].astype(F32) * given

        when(behind[o], add)


def local(
    centers,
    normals,
    weights,
    density,
    near_pairs,
    parent,
    far_src,
    src_basis,
    upward_transfer,
    far_mat,
    downward_transfer,
    tgt_basis,
):
    vmem = pl.BlockSpec(memory_space=pltpu.VMEM)
    smem = pl.BlockSpec(memory_space=pltpu.SMEM)
    dma = pltpu.SemaphoreType.DMA
    return pl.pallas_call(
        kernel,
        out_shape=jax.ShapeDtypeStruct((COLS, CL * PS), F32),
        in_specs=[vmem] * 4 + [smem] * 3 + [pl.BlockSpec(memory_space=pl.ANY)] * 5,
        out_specs=vmem,
        scratch_shapes=[
            pltpu.VMEM((CL, RANK, PS), BF16),
            pltpu.VMEM((CL, RANK, RANK), F32),
            pltpu.VMEM((TOPS * RANK, FAR * RANK), BF16),
            pltpu.VMEM((CL, RANK, RANK), F32),
            pltpu.VMEM((CL, RANK, PS), BF16),
            dma((5,)),
            pltpu.SMEM((64,), jnp.int32),
            pltpu.VMEM((CL, 8, PS), F32),
            pltpu.VMEM((CL, COLS, PS), BF16),
            pltpu.VMEM((HALF, PS, 128), BF16),
            pltpu.VMEM((HALF, 80, PS), BF16),
            pltpu.VMEM((COLS, HALF * PS), BF16),
            pltpu.VMEM((W, CAP, COLS, PS), BF16),
            pltpu.VMEM((W, 2, 16, PS), BF16),
            pltpu.VMEM((CAP, COLS, PS), BF16),
            pltpu.VMEM((CAP, COLS, PS), BF16),
            pltpu.VMEM((CAP, COLS, PS), BF16),
            pltpu.VMEM((CAP, COLS, PS), BF16),
            pltpu.VMEM((4, 16, PS), BF16),
            pltpu.VMEM((4, 16, PS), BF16),
            pltpu.VMEM((CAP, 80, PS), BF16),
            pltpu.VMEM((HALF, 2 * COLS, PS), F32),
            pltpu.VMEM((HALF, 2 * COLS, PS), F32),
            pltpu.VMEM((HALF, PS, PS), BF16),
            pltpu.VMEM((W, CAP, COLS, PS), F32),
            pltpu.VMEM((W, CAP, COLS, PS), F32),
            pltpu.VMEM((W, CAP, COLS, PS), F32),
            pltpu.VMEM((W, CAP, COLS, PS), BF16),
            pltpu.VMEM((CAP, COLS, PS), BF16),
            pltpu.VMEM((CAP, COLS, PS), BF16),
            pltpu.VMEM((HALF, COLS, PS), F32),
            pltpu.VMEM((HALF, COLS, PS), F32),
            pltpu.VMEM((2 * N, COLS, 128), BF16),
            pltpu.VMEM((TOPS * FAR, COLS, 128), BF16),
            pltpu.VMEM((TOPS, COLS, RANK), F32),
            pltpu.SMEM((128,), jnp.int32),
            pltpu.SMEM((128,), jnp.int32),
            pltpu.SMEM((128,), jnp.int32),
            pltpu.SMEM((128,), jnp.int32),
            pltpu.SMEM((HALF,), jnp.int32),
            pltpu.SMEM((HALF,), jnp.int32),
            dma((W,)), dma((W,)),
            dma, dma,
            dma((W, 2)), dma((W, 2)),
            dma((W,)), dma((W,)),
            dma((W, 2)), dma((W, 2)),
            dma((W,)), dma((W,)),
            dma((W, 2)), dma((W, 2)),
            dma((W, 2)), dma((W, 2)),
            dma, dma,
            dma((Z - 1,)), dma((Z - 1,)),
            dma((Y - 1,)), dma((Y - 1,)),
            dma((X - 1,)), dma((X - 1,)),
        ],
        compiler_params=pltpu.CompilerParams(
            collective_id=0, has_side_effects=True, vmem_limit_bytes=56 * 1024 * 1024
        ),
    )(
        centers,
        normals,
        weights,
        density,
        near_pairs,
        parent,
        far_src,
        src_basis,
        upward_transfer,
        far_mat.reshape(TOPS * RANK, FAR * RANK),
        downward_transfer,
        tgt_basis,
    )


def solution(mesh):
    placed = (
        P(None, "clus"),
        P(None, "clus"),
        P("clus"),
        P("rhs", "clus"),
        P(None, None, "clus"),
        P("clus"),
        P("clus", None),
        P("clus", None, None),
        P("clus", None, None),
        P("clus", None, None),
        P("clus", None, None),
        P("clus", None, None),
    )
    return jax.shard_map(
        local, mesh=mesh, in_specs=placed, out_specs=P("rhs", "clus"), check_vma=False
    )
```

```python
import functools

import jax
import jax.numpy as jnp
from jax import lax
from jax.experimental import pallas as pl
from jax.experimental.pallas import tpu as pltpu
from jax.sharding import PartitionSpec as P

F32 = jnp.float32
BF16 = jnp.bfloat16
MESH = pl.DeviceIdType.MESH
HIGHEST = lax.Precision.HIGHEST

DELTA2 = 0.25
W = 2
X, Z, Y = 4, 8, 4
N = X * Z * Y
CL = 16
HALF = 8
CAP = 8
PS = 512
COLS = 16
RANK = 32
TOPS = 8
FAR = 32

LIST, RANKED, PRESENT = 0, 8, 24
POWER, LOG = 0, 16
PRIME = 19


def mm(a, b, precision=None):
    return jnp.dot(a, b, preferred_element_type=F32, precision=precision)


def mm_nt(a, b, precision=None):
    return lax.dot_general(
        a, b, (((1,), (1,)), ((), ())), preferred_element_type=F32, precision=precision
    )


def split3(v):
    high = v.astype(BF16).astype(F32)
    rest = v - high
    mid = rest.astype(BF16).astype(F32)
    return high, mid, rest - mid


def features(geo):
    row = lax.broadcasted_iota(jnp.int32, geo.shape, 0)
    low = row < 3
    mid = (row >= 3) & (row < 6)
    w = geo[6:7]
    weighted = geo * w
    xh = weighted.astype(BF16).astype(F32)
    xl = weighted - xh
    yh = jnp.where(low, jnp.roll(xh, -3, axis=0), 0.0)
    yl = jnp.where(low, jnp.roll(xl, -3, axis=0), 0.0)
    c0, c1, c2 = geo[0:1], geo[1:2], geo[2:3]
    square = c0 * c0 + c1 * c1 + c2 * c2 + 0.5 * DELTA2
    offset = -(weighted[3:4] * c0 + weighted[4:5] * c1 + weighted[5:6] * c2)

    def rows_3_to_5(parts, base):
        h, m, l = parts
        return jnp.where(row == 3, h, jnp.where(row == 4, m, jnp.where(row == 5, l, base)))

    sh, sm, sl = split3(square)
    q1 = [
        rows_3_to_5((sh, sm, sl), jnp.where(low, -2.0 * geo, 0.0)),
        jnp.where(low, 1.0, 0.0),
    ]
    q2 = [
        jnp.where(low, geo, jnp.where(mid, 1.0, 0.0)),
        jnp.where(row == 0, sh, jnp.where(row == 1, sm, jnp.where(row == 2, sl, 0.0))),
    ]
    u = [jnp.where(low, xh, jnp.where(mid, w, 0.0)), xl, xh, xl]
    v = [rows_3_to_5(split3(offset), yh), yh, yl, yl]
    return q1, q2, u, v


def target_features(geo):
    q1, q2, u, v = features(geo)
    pad = jnp.zeros((48, PS), F32)
    left = jnp.concatenate(q1 + u + v + [pad], axis=0).T.astype(BF16)
    return left, jnp.concatenate(q2 + v + u, axis=0).astype(BF16)


def source_features(geo):
    q1, q2, u, v = features(geo)
    return jnp.concatenate(q2 + v + u, axis=0).astype(BF16)


def cube(q):
    t = lax.rsqrt(q)
    return t * t * t


def name_sources(pairs, o, small, idx):
    named = 0
    for p in range(CL):
        named = named | small[POWER + pairs[1, o, p]]
    before = 0
    for c in range(CL):
        present = (named >> c) & 1
        idx[RANKED + c] = before * present
        idx[PRESENT + c] = present
        before = before + present
    for m in range(CAP):
        lowest = named & (-named)
        idx[LIST + m] = small[LOG + lax.rem(lowest, PRIME)]
        named = named - lowest


def name_targets(pairs, o, mine, idx, slots):
    for t in range(HALF):
        source = 0
        for p in range(CL):
            source = source + jnp.where(pairs[0, o, p] == mine + t, pairs[1, o, p], 0)
        slots[t] = idx[RANKED + source]


def kernel(
    cen, nor, wts, den, pairs, parent, far_src, src_basis_hbm, up_hbm, far_mat_hbm, down_hbm,
    tgt_basis_hbm,
    out,
    src_basis, up, far_mat, down, tgt_basis, s_in,
    small, geo, dens, left, right, dsib, sendd, sendg, bown1, bown2, bsib1, bsib2, bgeo1, bgeo2,
    bright, near, ybuf, fbuf, part_own, part_sib, part_recv, ret_send, ret_recv1, ret_recv2,
    near_sib, near_recv, table, folded, far_top, idx1, idx2, ridx1, ridx2, slots1, slots2,
    s_idx, r_idx, s_sib, r_sib, s_bd, r_bd, s_bg, r_bg, s_fd, r_fd, s_fg, r_fg, s_ps, r_ps,
    s_rt, r_rt, s_nr, r_nr, s_z, r_z, s_y, r_y, s_x, r_x,
):
    me = lax.axis_index("clus")
    core = lax.axis_index("rhs")
    y = lax.rem(me, Y)
    z = lax.rem(me // Y, Z)
    x = me // (Y * Z)
    idx = (idx1, idx2)
    ridx = (ridx1, ridx2)
    slots = (slots1, slots2)
    bown, bsib, bgeo = (bown1, bown2), (bsib1, bsib2), (bgeo1, bgeo2)
    ret_recv = (ret_recv1, ret_recv2)
    mine = core * HALF
    other = (1 - core) * HALF

    ahead = [me + o + 1 < N for o in range(W)]
    behind = [me - o - 1 >= 0 for o in range(W)]

    def when(condition, *steps):
        @pl.when(condition)
        def _():
            for step in steps:
                step()

    def along(step):
        return {"clus": lax.rem(me + step + N, N)}

    sibling = {"rhs": 1 - core}
    z_peers = [{"clus": (x * Z + lax.rem(z + k, Z)) * Y + y} for k in range(1, Z)]
    y_peers = [{"clus": (x * Z + z) * Y + lax.rem(y + k, Y)} for k in range(1, Y)]
    x_peers = [{"clus": (lax.rem(x + k, X) * Z + z) * Y + y} for k in range(1, X)]

    def remote(src, dst, send, recv, to):
        return pltpu.make_async_remote_copy(
            src_ref=src, dst_ref=dst, send_sem=send, recv_sem=recv, device_id=to, device_id_type=MESH
        )

    barrier = pltpu.get_barrier_semaphore()
    partners = [sibling] + [along(s) for s in (1, 2, -1, -2)] + z_peers + y_peers + x_peers
    for partner in partners:
        pl.semaphore_signal(barrier, inc=1, device_id=partner, device_id_type=MESH)
    loads = [
        pltpu.make_async_copy(src, dst, s_in.at[k])
        for k, (src, dst) in enumerate(
            (
                (src_basis_hbm, src_basis),
                (up_hbm, up),
                (far_mat_hbm, far_mat),
                (down_hbm, down),
                (tgt_basis_hbm, tgt_basis),
            )
        )
    ]
    for load in loads:
        load.start()
    for c in range(CL):
        small[POWER + c] = 1 << c
    for p in range(PRIME):
        small[LOG + p] = 0
    for c in range(CL):
        small[LOG + (1 << c) % PRIME] = c
    for o in range(W):
        name_sources(pairs, o, small, idx[o])
    pl.semaphore_wait(barrier, len(partners))

    idx_copies = [
        remote(idx[o], ridx[o], s_idx.at[o], r_idx.at[o], along(o + 1)) for o in range(W)
    ]
    for o in range(W):
        when(ahead[o], idx_copies[o].start)
    sib_copy = remote(
        den.at[:, pl.ds(pl.multiple_of(other * PS, PS), HALF * PS)], dsib, s_sib, r_sib, sibling
    )
    sib_copy.start()

    for c in range(CL):
        at = pl.ds(c * PS, PS)
        w = wts[at].astype(F32).reshape(1, PS)
        rows = [cen[:, at].astype(F32), nor[:, at].astype(F32), w]
        dens[c] = den[:, at]
        geo[c] = jnp.concatenate(rows + [jnp.zeros((1, PS), F32)], axis=0)

    loads[0].wait()
    loads[1].wait()
    def blocks(wide):
        return [
            wide[c * COLS : (c + 1) * COLS, c * RANK : (c + 1) * RANK] for c in range(CL)
        ]

    leaf = mm_nt(dens[...].reshape(CL * COLS, PS), src_basis[...].reshape(CL * RANK, PS))
    leaf = jnp.concatenate(blocks(leaf), axis=0)
    tops = [jnp.zeros((COLS, RANK), F32) for _ in range(TOPS)]
    for c, child in enumerate(blocks(mm_nt(leaf, up[...].reshape(CL * RANK, RANK), HIGHEST))):
        for t in range(TOPS):
            tops[t] = tops[t] + jnp.where(parent[c] == t, child, 0.0)
    for h in range(2):
        table[2 * me + h] = jnp.concatenate(tops[4 * h : 4 * h + 4], axis=1).astype(BF16)

    def gather_step(start, size, peers, send, recv):
        block = table.at[pl.ds(start, size)]
        copies = [
            remote(block, block, send.at[k], recv.at[k], to) for k, to in enumerate(peers)
        ]
        for copy in copies:
            copy.start()
        return copies

    y_copies = gather_step(2 * me, 2, y_peers, s_y, r_y)

    b_copies = []
    for o in range(W):

        def gather(o=o):
            idx_copies[o].wait_recv()
            for m in range(CAP):
                sendd[o, m] = dens[ridx[o][LIST + m]]
            for m in range(2):
                c0 = ridx[o][LIST + core * 4 + 2 * m]
                c1 = ridx[o][LIST + core * 4 + 2 * m + 1]
                sendg[o, m] = jnp.concatenate([geo[c0], geo[c1]], axis=0).astype(BF16)

        when(behind[o], gather)
        half = pl.ds(core * 2, 2)
        copies = (
            remote(sendg.at[o], bgeo[o].at[half], s_bg.at[o], r_bg.at[o], along(-o - 1)),
            *(
                remote(
                    sendd.at[o, pl.ds(4 * h, 4)], bown[o].at[pl.ds(4 * h, 4)],
                    s_bd.at[o, h], r_bd.at[o, h], along(-o - 1),
                )
                for h in range(2)
            ),
        )
        b_copies.append(copies)
        if o == 0:
            when(behind[o], *(copy.start for copy in copies))

    for t in range(HALF):
        left[t], right[t] = target_features(geo[mine + t])
    for copy in y_copies:
        copy.wait()
    z_copies = gather_step((x * Z + z) * Y * 2, Y * 2, z_peers, s_z, r_z)
    sib_copy.wait()
    for o in range(W):
        name_targets(pairs, o, mine, idx[o], slots[o])

    def densities(t):
        own = den[:, pl.ds(pl.multiple_of((mine + t) * PS, PS), PS)]
        return jnp.concatenate([own, dsib[:, pl.ds(pl.multiple_of(t * PS, PS), PS)]], axis=0)

    def self_pair(u, carry):
        for k in range(2):
            t = 2 * u + k
            q = mm(left[t, :, 0:16], right[t, 0:16])
            nb = mm(left[t, :, 48:80], right[t, 48:80])
            near[t] = mm(densities(t), (nb * cube(q)).astype(BF16))
        return carry

    lax.fori_loop(0, HALF // 4, self_pair, 0)

    when(behind[1], *(copy.start for copy in b_copies[1]))
    for copy in z_copies:
        copy.wait()
    x_copies = gather_step(x * Y * Z * 2, Y * Z * 2, x_peers, s_x, r_x)

    def arrived(o):
        half = pl.ds(core * 2, 2)
        forwards = [remote(bgeo[o].at[half], bgeo[o].at[half], s_fg.at[o], r_fg.at[o], sibling)]
        for h in range(2):
            part = pl.ds(4 * h, 4)
            forwards.append(
                remote(bown[o].at[part], bsib[o].at[part], s_fd.at[o, h], r_fd.at[o, h], sibling)
            )

        def pass_on():
            for arrival, forward in zip(b_copies[o], forwards):
                arrival.wait_recv()
                forward.start()

        when(ahead[o], pass_on)
        when(behind[o], *(copy.wait_send for copy in b_copies[o]))
        return forwards

    def prepare(o, forwards):
        when(ahead[o], *(copy.wait for copy in forwards))
        for m in range(CAP):
            pair = bgeo[o][m // 2].astype(F32)
            bright[m] = source_features(pair[8 * (m % 2) : 8 * (m % 2) + 8])

    def cross(o, first, last, later):
        def cross_pair(u, carry):
            for k in range(4):
                t = 4 * u + k
                m = slots[o][t]
                q = mm(left[t, :, 0:16], bright[m, 0:16])
                nf = mm(left[t, :, 16:48], bright[m, 16:48])
                nb = mm(left[t, :, 48:80], bright[m, 48:80])
                scale = cube(q)
                ybuf[t] = mm(densities(t), (nb * scale).astype(BF16))
                if later:
                    fbuf[t] = (nf * scale).astype(BF16)
                else:
                    there = jnp.concatenate([bown[o][m], bsib[o][m]], axis=0)
                    there = mm_nt(there, (nf * scale).astype(BF16))
                    near[t] += jnp.where(ahead[o], there, 0.0)
            return carry

        lax.fori_loop(first // 4, last // 4, cross_pair, 0)

    def cross_rest(o):
        def rest_pair(u, carry):
            for k in range(2):
                t = 2 * u + k
                m = slots[o][t]
                there = jnp.concatenate([bown[o][m], bsib[o][m]], axis=0)
                near[t] += jnp.where(ahead[o], mm_nt(there, fbuf[t]), 0.0)
            return carry

        lax.fori_loop(0, HALF // 2, rest_pair, 0)

    def share(o):
        copies = []
        for h in range(2):
            for rows, dst in ((COLS, part_sib), (0, part_own)):
                for r in range(0, COLS, 8):
                    tiles = [ybuf[t, rows + r : rows + r + 8, :] for t in range(HALF)]
                    for m in range(4 * h, 4 * h + 4):
                        total = None
                        for t in range(HALF):
                            hit = jnp.where(slots[o][t] == m, 1.0, 0.0).astype(F32)
                            term = hit * tiles[t]
                            total = term if total is None else total + term
                        dst[o, m, r : r + 8, :] = total
                if rows == COLS:
                    part = pl.ds(4 * h, 4)
                    copies.append(
                        remote(
                            part_sib.at[o, part], part_recv.at[o, part],
                            s_ps.at[o, h], r_ps.at[o, h], sibling,
                        )
                    )
                    copies[-1].start()
        return copies

    def send_back(o, copies):
        returned = []
        for h in range(2):
            copies[h].wait()
            for m in range(4 * h, 4 * h + 4):
                ret_send[o, m] = (part_own[o, m] + part_recv[o, m]).astype(BF16)
            part = pl.ds(4 * h, 4)
            returned.append(
                remote(
                    ret_send.at[o, part], ret_recv[o].at[part],
                    s_rt.at[o, h], r_rt.at[o, h], along(o + 1),
                )
            )
            when(ahead[o], returned[-1].start)
        return returned

    forwards = arrived(0)
    lax.fori_loop(HALF // 4, HALF // 2, self_pair, 0)
    prepare(0, forwards)
    cross(0, 0, 4, False)
    forwards = arrived(1)
    cross(0, 4, 8, False)
    part = share(0)
    prepare(1, forwards)
    cross(1, 0, 4, True)
    backs = [send_back(0, part)]
    cross(1, 4, 8, True)
    part = share(1)
    cross_rest(1)
    backs.append(send_back(1, part))
    for t in range(HALF):
        near_sib[t] = near[t, COLS:, :]
    near_copy = remote(near_sib, near_recv, s_nr, r_nr, sibling)
    near_copy.start()

    for load in loads[2:]:
        load.wait()
    for copy in x_copies:
        copy.wait()
    lane = lax.broadcasted_iota(jnp.int32, (COLS, 128), 1) // RANK
    for t in range(TOPS):
        for f in range(FAR):
            top = far_src[t, f]
            tile = table[top >> 2].astype(F32)
            folded[t * FAR + f] = jnp.where(lane == (top & 3), tile, 0.0).astype(BF16)
    ones_row = lax.rem(lax.broadcasted_iota(jnp.int32, (128, 128), 0), RANK)
    ones_col = lax.rem(lax.broadcasted_iota(jnp.int32, (128, 128), 1), RANK)
    spread = jnp.where(ones_row == ones_col, 1.0, 0.0).astype(BF16)
    picked = []
    for t in range(TOPS):
        tiles = folded[t * FAR : (t + 1) * FAR].reshape(FAR * COLS, 128)
        everywhere = mm(tiles, spread)
        groups = []
        for g in range(FAR // 4):
            total = None
            for k in range(4):
                f = 4 * g + k
                term = jnp.where(lane == k, everywhere[f * COLS : (f + 1) * COLS], 0.0)
                total = term if total is None else total + term
            groups.append(total.astype(BF16))
        picked.append(jnp.concatenate(groups, axis=1))
    distant = mm_nt(jnp.concatenate(picked, axis=0), far_mat[...])
    for t in range(TOPS):
        far_top[t] = distant[t * COLS : (t + 1) * COLS, t * RANK : (t + 1) * RANK]
    upper = jnp.concatenate([far_top[parent[c]] for c in range(CL)], axis=0)
    lower = mm_nt(upper, down[...].reshape(CL * RANK, RANK), HIGHEST)
    same = lax.broadcasted_iota(jnp.int32, lower.shape, 0) // COLS == (
        lax.broadcasted_iota(jnp.int32, lower.shape, 1) // RANK
    )
    lower = jnp.where(same, lower, 0.0).astype(BF16)
    far_part = mm(lower, tgt_basis[...].reshape(CL * RANK, PS))
    for c in range(CL):
        out[:, c * PS : (c + 1) * PS] = far_part[c * COLS : (c + 1) * COLS]

    near_copy.wait()
    for t in range(HALF):
        at = pl.ds(pl.multiple_of((mine + t) * PS, PS), PS)
        out[:, at] += near[t, 0:COLS, :]
        at = pl.ds(pl.multiple_of((other + t) * PS, PS), PS)
        out[:, at] += near_recv[t]
    for o in range(W):
        when(ahead[o], idx_copies[o].wait_send, *(copy.wait_send for copy in backs[o]))

        def add(o=o):
            for copy in backs[o]:
                copy.wait_recv()
            for c in range(CL):
                at = pl.ds(c * PS, PS)
                given = ret_recv[o][ridx[o][RANKED + c]].astype(F32)
                out[:, at] += ridx[o][PRESENT + c].astype(F32) * given

        when(behind[o], add)


def local(
    centers,
    normals,
    weights,
    density,
    near_pairs,
    parent,
    far_src,
    src_basis,
    upward_transfer,
    far_mat,
    downward_transfer,
    tgt_basis,
):
    vmem = pl.BlockSpec(memory_space=pltpu.VMEM)
    smem = pl.BlockSpec(memory_space=pltpu.SMEM)
    dma = pltpu.SemaphoreType.DMA
    return pl.pallas_call(
        kernel,
        out_shape=jax.ShapeDtypeStruct((COLS, CL * PS), F32),
        in_specs=[vmem] * 4 + [smem] * 3 + [pl.BlockSpec(memory_space=pl.ANY)] * 5,
        out_specs=vmem,
        scratch_shapes=[
            pltpu.VMEM((CL, RANK, PS), BF16),
            pltpu.VMEM((CL, RANK, RANK), F32),
            pltpu.VMEM((TOPS * RANK, FAR * RANK), BF16),
            pltpu.VMEM((CL, RANK, RANK), F32),
            pltpu.VMEM((CL, RANK, PS), BF16),
            dma((5,)),
            pltpu.SMEM((64,), jnp.int32),
            pltpu.VMEM((CL, 8, PS), F32),
            pltpu.VMEM((CL, COLS, PS), BF16),
            pltpu.VMEM((HALF, PS, 128), BF16),
            pltpu.VMEM((HALF, 80, PS), BF16),
            pltpu.VMEM((COLS, HALF * PS), BF16),
            pltpu.VMEM((W, CAP, COLS, PS), BF16),
            pltpu.VMEM((W, 2, 16, PS), BF16),
            pltpu.VMEM((CAP, COLS, PS), BF16),
            pltpu.VMEM((CAP, COLS, PS), BF16),
            pltpu.VMEM((CAP, COLS, PS), BF16),
            pltpu.VMEM((CAP, COLS, PS), BF16),
            pltpu.VMEM((4, 16, PS), BF16),
            pltpu.VMEM((4, 16, PS), BF16),
            pltpu.VMEM((CAP, 80, PS), BF16),
            pltpu.VMEM((HALF, 2 * COLS, PS), F32),
            pltpu.VMEM((HALF, 2 * COLS, PS), F32),
            pltpu.VMEM((HALF, PS, PS), BF16),
            pltpu.VMEM((W, CAP, COLS, PS), F32),
            pltpu.VMEM((W, CAP, COLS, PS), F32),
            pltpu.VMEM((W, CAP, COLS, PS), F32),
            pltpu.VMEM((W, CAP, COLS, PS), BF16),
            pltpu.VMEM((CAP, COLS, PS), BF16),
            pltpu.VMEM((CAP, COLS, PS), BF16),
            pltpu.VMEM((HALF, COLS, PS), F32),
            pltpu.VMEM((HALF, COLS, PS), F32),
            pltpu.VMEM((2 * N, COLS, 128), BF16),
            pltpu.VMEM((TOPS * FAR, COLS, 128), BF16),
            pltpu.VMEM((TOPS, COLS, RANK), F32),
            pltpu.SMEM((128,), jnp.int32),
            pltpu.SMEM((128,), jnp.int32),
            pltpu.SMEM((128,), jnp.int32),
            pltpu.SMEM((128,), jnp.int32),
            pltpu.SMEM((HALF,), jnp.int32),
            pltpu.SMEM((HALF,), jnp.int32),
            dma((W,)), dma((W,)),
            dma, dma,
            dma((W, 2)), dma((W, 2)),
            dma((W,)), dma((W,)),
            dma((W, 2)), dma((W, 2)),
            dma((W,)), dma((W,)),
            dma((W, 2)), dma((W, 2)),
            dma((W, 2)), dma((W, 2)),
            dma, dma,
            dma((Z - 1,)), dma((Z - 1,)),
            dma((Y - 1,)), dma((Y - 1,)),
            dma((X - 1,)), dma((X - 1,)),
        ],
        compiler_params=pltpu.CompilerParams(
            collective_id=0, has_side_effects=True, vmem_limit_bytes=56 * 1024 * 1024
        ),
    )(
        centers,
        normals,
        weights,
        density,
        near_pairs,
        parent,
        far_src,
        src_basis,
        upward_transfer,
        far_mat.reshape(TOPS * RANK, FAR * RANK),
        downward_transfer,
        tgt_basis,
    )


def solution(mesh):
    placed = (
        P(None, "clus"),
        P(None, "clus"),
        P("clus"),
        P("rhs", "clus"),
        P(None, None, "clus"),
        P("clus"),
        P("clus", None),
        P("clus", None, None),
        P("clus", None, None),
        P("clus", None, None),
        P("clus", None, None),
        P("clus", None, None),
    )
    return jax.shard_map(
        local, mesh=mesh, in_specs=placed, out_specs=P("rhs", "clus"), check_vma=False
    )
```
